32 devices in a mesh: narrow: 4 (over y, core), wide: 8 (over z, x).
Axes of the slice: x: 2, y: 2, z: 4, core: 2. Of those that a mesh axis runs over, the one named last changes fastest.
Arguments:
- adjoint_hat: float32 [3, 2, 256, 256, 256], P(None, None, 'wide', 'narrow'), may hold values from -3 to 3
- velocity_hat: float32 [3, 2, 256, 256, 256], P(None, None, 'wide', 'narrow'), may hold values from -3 to 3
Outputs:
- adjoint_next: float32 [3, 2, 256, 256, 256], P(None, None, 'wide', 'narrow')
The draws below stay inside these ranges and needn't reach their ends.
All inputs are finite; a program needn't handle non-finite values.
Results may differ from the reference program's by a relative error of at most 0.00005.
Values sent between devices are 32-bit elements; how exact they have to be, the bound alone decides.
A program may use at most 256 MiB of HBM per device.

```python
import math
import jax
import jax.numpy as jnp
from jax import lax

NX = 512
NY = 256
NZ = 256
KX = 256


def steps_of(stream_key, extent, pieces, smallest, largest):
    def one(axis_at, parts):
        steps = jax.random.uniform(jax.random.fold_in(jax.random.fold_in(stream_key, 6), axis_at), (parts,), jnp.float32, smallest / len(pieces), largest / len(pieces))
        return jnp.repeat(jnp.exp(steps), extent[axis_at] // parts).reshape((-1,) + (1,) * (len(extent) - axis_at - 1))

    level = one(*pieces[0])
    for cut in pieces[1:]:
        level = level * one(*cut)
    return level


def gaussian(rng, extent, deviation, bound, shards=(), kind=jnp.bfloat16):
    loudness = steps_of(rng, extent, shards, -0.22, 0.18) if shards else 1.0
    entries = jax.random.normal(rng, extent, jnp.float32) * deviation * loudness
    return jnp.minimum(jnp.maximum(entries, -bound), bound).astype(kind)


def setup_inputs(seed: int = 0) -> dict:
    keys = jax.random.split(jax.random.key(seed), 3)
    adjoint_hat = gaussian(keys[0], (3, 2, KX, NY, NZ), 0.5, 3.0, ((2, 8), (3, 4)), jnp.float32)
    velocity_hat = gaussian(keys[1], (3, 2, KX, NY, NZ), 0.5, 3.0, ((2, 8), (3, 4)), jnp.float32)
    return dict(adjoint_hat=adjoint_hat, velocity_hat=velocity_hat)


def signed_modes(length):
    number = jnp.arange(length, dtype=jnp.int32)
    return jnp.where(number < length // 2, number, number - length)


def synthesize(real_part, imag_part):
    spectra = lax.complex(real_part, imag_part)
    spectra = jnp.fft.ifft(spectra, axis=2, norm="ortho")
    spectra = jnp.fft.ifft(spectra, axis=1, norm="ortho")
    weights = jnp.where(jnp.arange(KX, dtype=jnp.int32) == 0, 1.0, 2.0).astype(real_part.dtype)[:, None, None]
    spectra = spectra * weights
    padded = jnp.concatenate([spectra, jnp.zeros((NX - KX, NY, NZ), spectra.dtype)], axis=0)
    return jnp.real(jnp.fft.ifft(padded, axis=0, norm="ortho"))


def analyze(field):
    spectra = jnp.fft.rfft(field, axis=0, norm="ortho")[:KX]
    spectra = jnp.fft.fft(spectra, axis=1, norm="ortho")
    spectra = jnp.fft.fft(spectra, axis=2, norm="ortho")
    return jnp.real(spectra), jnp.imag(spectra)


def cross_list(first, second):
    return [first[1] * second[2] - first[2] * second[1],
            first[2] * second[0] - first[0] * second[2],
            first[0] * second[1] - first[1] * second[0]]


def reference(adjoint_hat, velocity_hat):
    number_x = jnp.arange(KX, dtype=jnp.int32)[:, None, None]
    number_y = signed_modes(NY)[None, :, None]
    number_z = signed_modes(NZ)[None, None, :]
    waves = [(2.0 * math.pi / NX) * number_x.astype(jnp.float32),
             (2.0 * math.pi / NY) * number_y.astype(jnp.float32),
             (2.0 * math.pi / NZ) * number_z.astype(jnp.float32)]
    vel_real = [velocity_hat[c, 0] for c in range(3)]
    vel_imag = [velocity_hat[c, 1] for c in range(3)]
    vort_real = [-v for v in cross_list(waves, vel_imag)]
    vort_imag = cross_list(waves, vel_real)
    adjoint = [synthesize(adjoint_hat[c, 0], adjoint_hat[c, 1]) for c in range(3)]
    velocity = [synthesize(vel_real[c], vel_imag[c]) for c in range(3)]
    vorticity = [synthesize(vort_real[c], vort_imag[c]) for c in range(3)]
    rotation = [analyze(g) for g in cross_list(adjoint, vorticity)]
    transport = [analyze(g) for g in cross_list(velocity, adjoint)]
    curl_real = cross_list(waves, [t[1] for t in transport])
    curl_imag = cross_list(waves, [t[0] for t in transport])
    conv_real = [rotation[c][0] - curl_real[c] for c in range(3)]
    conv_imag = [rotation[c][1] + curl_imag[c] for c in range(3)]
    keep = ((3 * number_x < NX) & (3 * jnp.abs(number_y) < NY) & (3 * jnp.abs(number_z) < NZ)).astype(jnp.float32)
    ksq = waves[0] ** 2 + waves[1] ** 2 + waves[2] ** 2
    divisor = ksq + (ksq == 0).astype(jnp.float32)
    decay = jnp.exp(-0.05 * ksq)
    results = []
    for conv in (conv_real, conv_imag):
        along = (waves[0] * conv[0] + waves[1] * conv[1] + waves[2] * conv[2]) / divisor
        results.append([keep * (conv[c] - waves[c] * along) for c in range(3)])
    output = []
    for c in range(3):
        output.append(jnp.stack([decay * (adjoint_hat[c, 0] + 0.25 * results[0][c]),
                                 decay * (adjoint_hat[c, 1] + 0.25 * results[1][c])], 0))
    return jnp.stack(output, 0)
```

```python
import functools
import math

import jax
import jax.numpy as jnp
import ml_dtypes
import numpy as np
from jax import lax
from jax.experimental import pallas as pl
from jax.experimental.pallas import tpu as pltpu
from jax.sharding import PartitionSpec as P

NX = 512
NY = 256
NZ = 256
KX = 256

section_step = 0.25
viscous_rate = 0.05
axes = ("wide", "narrow")
VMEM_LIMIT = 60 * 2**20


def signed(count):
    number = np.arange(count)
    return np.where(number < count // 2, number, number - count).astype(np.float64)


def phases(modes, places, length):
    angle = 2.0 * math.pi / length * (np.outer(np.arange(modes), np.arange(places)) % length)
    return np.cos(angle), np.sin(angle)


def split_table(table):
    table = np.asarray(table, np.float32)
    high = table.astype(ml_dtypes.bfloat16)
    low = (table - high.astype(np.float32)).astype(ml_dtypes.bfloat16)
    return np.stack([high, low], 0)


def split(value):
    high = value.astype(jnp.bfloat16)
    return high, (value - high.astype(jnp.float32)).astype(jnp.bfloat16)


def product(left, right, dims):
    def one(first, second):
        return lax.dot_general(first, second, (dims, ((), ())), preferred_element_type=jnp.float32)

    return one(left[1], right[0]) + one(left[0], right[1]) + one(left[0], right[0])


def table_parts(ref):
    return ref[0], ref[1]


PLAIN = ((1,), (0,))
BOTH_MINOR = ((1,), (1,))


def whole_spec(shape):
    return pl.BlockSpec(shape, lambda *_: (0,) * len(shape), pipeline_mode=pl.Buffered(1))


def params():
    return pltpu.CompilerParams(vmem_limit_bytes=VMEM_LIMIT)


def cost(flops, moved):
    return pl.CostEstimate(flops=int(flops), bytes_accessed=int(moved), transcendentals=0)


def depth_kernel(tables_count, by_owner, field_ref, *refs):
    tables, outs = refs[:tables_count], refs[tables_count:]
    for row in range(field_ref.shape[2]):
        real, imag = field_ref[0, 0, row], field_ref[0, 1, row]
        first = jnp.concatenate([real, imag], 0)
        second = jnp.concatenate([-imag, real], 0)
        rows = split(jnp.concatenate([first, second], 1))
        for table, out in zip(tables, outs):
            value = product(table_parts(table), rows, BOTH_MINOR)
            if by_owner:
                out[:, row] = value.reshape(out.shape[0], out.shape[2], out.shape[3])
            else:
                out[row] = value


def depth(field, member, tables, owners):
    rows_x, rows_y = field.shape[2], field.shape[3]
    block = NZ // owners
    lanes = 2 * rows_y
    tile = min(8, rows_x)
    by_owner = block % 8 == 0
    if by_owner:
        shape = (owners, rows_x, block, lanes)
        spec = pl.BlockSpec((owners, tile, block, lanes), lambda i: (0, i, 0, 0))
    else:
        shape = (rows_x, NZ, lanes)
        spec = pl.BlockSpec((tile, NZ, lanes), lambda i: (i, 0, 0))
    count = len(tables)
    outs = pl.pallas_call(
        functools.partial(depth_kernel, count, by_owner),
        grid=(rows_x // tile,),
        in_specs=[pl.BlockSpec((1, 2, tile, rows_y, NZ), lambda i: (member, 0, i, 0, 0))]
        + [whole_spec(t.shape) for t in tables],
        out_specs=[spec] * count,
        out_shape=[jax.ShapeDtypeStruct(shape, jnp.float32)] * count,
        compiler_params=params(),
        cost_estimate=cost(6.0 * count * rows_x * lanes * NZ * 2 * NZ, 4 * (count + 1) * rows_x * lanes * NZ),
        name="depth_synthesis",
    )(field, *tables)
    if not by_owner:
        outs = [o.reshape(rows_x, owners, block, lanes).transpose(1, 0, 2, 3) for o in outs]
    return outs


def exchange(value):
    return lax.all_to_all(value, axes, split_axis=0, concat_axis=0, tiled=True)


def plane_rows(ref, narrow, block, plane):
    owners, rows, lanes = ref.shape
    value = ref[:, pl.ds(plane, rows // block, stride=block), :]
    value = value.reshape(owners // narrow, narrow, rows // block, lanes)
    pieces = [value[:, n].reshape(KX, lanes) for n in range(narrow)]
    return split(jnp.concatenate(pieces, 1))


def stacked(value):
    return jnp.concatenate([value[:, :NY], value[:, NY:]], 0)


def times_i(value):
    return jnp.concatenate([-value[:, NY:], value[:, :NY]], 1)


def lines(value, synth):
    return product(table_parts(synth), split(stacked(value)), PLAIN)


def velocity_kernel(narrow, block, *refs):
    ux, uy, uz, dzux, dzuy, span, slope, synth = refs[:8]
    outs = refs[8:]
    plane = pl.program_id(0)
    wave = lax.broadcasted_iota(jnp.int32, (KX, 2 * NY), 0).astype(jnp.float32) * (2.0 * math.pi / NX)

    def rows(ref):
        return plane_rows(ref, narrow, block, plane)

    def to_y(value, table):
        return product(value, table_parts(table), PLAIN)

    rows_x = rows(ux)
    value_x = to_y(rows_x, span)
    outs[0][0] = lines(value_x, synth)
    value_y = to_y(rows(uy), span)
    outs[1][0] = lines(value_y, synth)
    rows_z = rows(uz)
    value_z = to_y(rows_z, span)
    outs[2][0] = lines(value_z, synth)
    outs[3][0] = lines(to_y(rows_z, slope) - to_y(rows(dzuy), span), synth)
    outs[4][0] = lines(to_y(rows(dzux), span) - wave * times_i(value_z), synth)
    outs[5][0] = lines(wave * times_i(value_y) - to_y(rows_x, slope), synth)


def adjoint_kernel(narrow, block, field, span, synth, out):
    rows = plane_rows(field, narrow, block, pl.program_id(0))
    out[0] = lines(product(rows, table_parts(span), PLAIN), synth)


def physical_call(kernel, name, fields, tables, count, narrow):
    owners, rows_x, block, lanes = fields[0].shape
    fields = [f.reshape(owners, rows_x * block, lanes) for f in fields]
    spec = pl.BlockSpec((1, NX, NY), lambda z: (z, 0, 0))
    return pl.pallas_call(
        functools.partial(kernel, narrow, block),
        grid=(block,),
        in_specs=[whole_spec(f.shape) for f in fields] + [whole_spec(t.shape) for t in tables],
        out_specs=[spec] * count,
        out_shape=[jax.ShapeDtypeStruct((block, NX, NY), jnp.float32)] * count,
        compiler_params=params(),
        cost_estimate=cost(12.0 * count * block * KX * 4 * NY * NY, 4 * 2 * count * block * NX * NY),
        name=name,
    )(*fields, *tables)


def analysis_kernel(kept, rows_x, narrow, *refs):
    a = [r[0] for r in refs[0:3]]
    u = [r[0] for r in refs[3:6]]
    o = [r[0] for r in refs[6:9]]
    anal, span, slope = refs[9:12]
    outs = refs[12:]
    wave = lax.broadcasted_iota(jnp.int32, (kept, 2 * NY), 0).astype(jnp.float32) * (2.0 * math.pi / NX)

    def cross(p, q, c):
        d, e = (c + 1) % 3, (c + 2) % 3
        return p[d] * q[e] - p[e] * q[d]

    def modes(cells):
        value = product(table_parts(anal), split(cells), PLAIN)
        return jnp.concatenate([value[:kept], value[kept:]], 1)

    def to_y(value, table):
        return product(split(value), table_parts(table), PLAIN)

    def store(out, value):
        lanes = value.shape[1] // narrow
        for w in range(kept // rows_x):
            for n in range(narrow):
                out[w * narrow + n, 0] = value[w * rows_x : (w + 1) * rows_x, n * lanes : (n + 1) * lanes]
        for d in range(kept // rows_x * narrow, out.shape[0]):
            out[d, 0] = jnp.zeros(out.shape[2:], jnp.float32)

    tx, ty, tz = [modes(cross(u, a, c)) for c in range(3)]
    store(outs[3], to_y(tx, span))
    store(outs[4], to_y(ty, span))
    store(outs[0], to_y(modes(cross(a, o, 0)), span) + to_y(tz, slope))
    store(outs[1], to_y(modes(cross(a, o, 1)) - wave * times_i(tz), span))
    store(outs[2], to_y(modes(cross(a, o, 2)) + wave * times_i(ty), span) - to_y(tx, slope))


def analysis(fields, tables, kept, rows_x, wide, narrow):
    block = fields[0].shape[0]
    owners = wide * narrow
    lanes = 2 * NY // narrow
    spec = pl.BlockSpec((1, NX, NY), lambda z: (z, 0, 0))
    out = pl.BlockSpec((owners, 1, rows_x, lanes), lambda z: (0, z, 0, 0))
    return pl.pallas_call(
        functools.partial(analysis_kernel, kept, rows_x, narrow),
        grid=(block,),
        in_specs=[spec] * 9 + [whole_spec(t.shape) for t in tables],
        out_specs=[out] * 5,
        out_shape=[jax.ShapeDtypeStruct((owners, block, rows_x, lanes), jnp.float32)] * 5,
        compiler_params=params(),
        cost_estimate=cost(6.0 * block * 13 * kept * 2 * NX * NY, 4 * 14 * block * NX * NY),
        name="products_and_analysis",
    )(*fields, *tables)


def final_kernel(*refs):
    spectra, adjoint, table, out = refs[:5], refs[5], refs[6], refs[7]
    tile, rows_y = adjoint.shape[2], adjoint.shape[3]
    first_x = lax.axis_index("wide") * (tile * pl.num_programs(0)) + pl.program_id(0) * tile
    shape = (rows_y, NZ)
    number_y = lax.broadcasted_iota(jnp.int32, shape, 0) + lax.axis_index("narrow") * rows_y
    number_y = jnp.where(number_y < NY // 2, number_y, number_y - NY)
    number_z = lax.broadcasted_iota(jnp.int32, shape, 1)
    number_z = jnp.where(number_z < NZ // 2, number_z, number_z - NZ)
    keep_yz = (3 * jnp.abs(number_y) < NY) & (3 * jnp.abs(number_z) < NZ)
    ky = number_y.astype(jnp.float32) * (2.0 * math.pi / NY)
    kz = number_z.astype(jnp.float32) * (2.0 * math.pi / NZ)
    for row in range(tile):
        parts = []
        for ref in spectra:
            flat = ref.reshape(NZ * tile, 2 * rows_y)
            cells = flat[pl.ds(row, NZ, stride=tile), :].T
            both = product(split(cells), table_parts(table), PLAIN)
            cosine, sine = both[:, :NZ], both[:, NZ:]
            parts.append((cosine[:rows_y] + sine[rows_y:], cosine[rows_y:] - sine[:rows_y]))
        number_x = jnp.full(shape, first_x + row, jnp.int32)
        kx = number_x.astype(jnp.float32) * (2.0 * math.pi / NX)
        ksquare = kx * kx + ky * ky + kz * kz
        inverse = 1.0 / (ksquare + (ksquare == 0).astype(jnp.float32))
        keep = (keep_yz & (3 * number_x < NX)).astype(jnp.float32) * section_step
        decay = jnp.exp(-viscous_rate * ksquare)
        a1, a2, a3, t1, t2 = parts
        real = (a1[0] + kz * t2[1], a2[0] - kz * t1[1], a3[0])
        imag = (a1[1] - kz * t2[0], a2[1] + kz * t1[0], a3[1])
        for part, conv in enumerate((real, imag)):
            along = (kx * conv[0] + ky * conv[1] + kz * conv[2]) * inverse
            for c, wave in enumerate((kx, ky, kz)):
                out[c, part, row] = decay * (adjoint[c, part, row] + keep * (conv[c] - wave * along))


def final(spectra, adjoint_hat, table):
    rows_x, rows_y = adjoint_hat.shape[2], adjoint_hat.shape[3]
    tile = min(8, rows_x)
    spectra = [s.reshape(NZ, rows_x, 2 * rows_y) for s in spectra]
    hat = pl.BlockSpec((3, 2, tile, rows_y, NZ), lambda i: (0, 0, i, 0, 0))
    return pl.pallas_call(
        final_kernel,
        grid=(rows_x // tile,),
        in_specs=[pl.BlockSpec((NZ, tile, 2 * rows_y), lambda i: (0, i, 0))] * 5 + [hat, whole_spec(table.shape)],
        out_specs=hat,
        out_shape=jax.ShapeDtypeStruct(adjoint_hat.shape, jnp.float32),
        compiler_params=params(),
        cost_estimate=cost(30.0 * rows_x * 2 * rows_y * NZ * 2 * NZ, 4 * 22 * rows_x * rows_y * NZ),
        name="depth_analysis_projection",
    )(*spectra, adjoint_hat, table)


def local(wide, narrow, adjoint_hat, velocity_hat):
    owners = wide * narrow
    rows_x, rows_y = adjoint_hat.shape[2], adjoint_hat.shape[3]
    kept = -(-(-(-NX // 3)) // rows_x) * rows_x
    scale = 1.0 / math.sqrt(NX * NY * NZ)
    cosine, sine = phases(NZ, NZ, NZ)
    wave_z = 2.0 * math.pi / NZ * signed(NZ)[None, :]
    depth_table = split_table(np.concatenate([cosine, sine], 1))
    depth_slope = split_table(np.concatenate([-wave_z * sine, wave_z * cosine], 1))
    final_table = split_table(np.concatenate([cosine, sine], 1))
    cosine, sine = phases(NY, NY, NY)
    wave_y = 2.0 * math.pi / NY * signed(NY)[:, None]

    def merged(real, imag):
        return np.stack([np.stack([real, imag], 1), np.stack([-imag, real], 1)], 0)

    def rows_first(real, imag):
        table = merged(real, imag).reshape(2, narrow, rows_y, 2, NY)
        return split_table(table.transpose(1, 0, 2, 3, 4).reshape(2 * NY, 2 * NY))

    def rows_last(real, imag):
        table = merged(real, imag).transpose(0, 3, 2, 1).reshape(2, NY, 2, narrow, rows_y)
        return split_table(table.transpose(0, 1, 3, 2, 4).reshape(2 * NY, 2 * NY))

    span = rows_first(cosine, sine)
    slope = rows_first(-wave_y * sine, wave_y * cosine)
    back_span = rows_last(cosine, -sine)
    back_slope = rows_last(wave_y * sine, wave_y * cosine)
    cosine, sine = phases(KX, NX, NX)
    weights = np.where(np.arange(KX) == 0, 1.0, 2.0)[:, None] * scale
    synth = split_table(np.concatenate([cosine * weights, -sine * weights], 0).T)
    anal = split_table(np.concatenate([cosine[:kept], -sine[:kept]], 0) * scale)

    ux, dzux = [exchange(v) for v in depth(velocity_hat, 0, [depth_table, depth_slope], owners)]
    uy, dzuy = [exchange(v) for v in depth(velocity_hat, 1, [depth_table, depth_slope], owners)]
    uz = exchange(depth(velocity_hat, 2, [depth_table], owners)[0])
    hats = [exchange(depth(adjoint_hat, c, [depth_table], owners)[0]) for c in range(3)]
    flow = physical_call(
        velocity_kernel, "velocity_lines", [ux, uy, uz, dzux, dzuy], [span, slope, synth], 6, narrow
    )
    adjoint = [
        physical_call(adjoint_kernel, "adjoint_lines", [hat], [span, synth], 1, narrow)[0] for hat in hats
    ]
    spectra = analysis(
        adjoint + list(flow), [anal, back_span, back_slope], kept, rows_x, wide, narrow
    )
    return final([exchange(s) for s in spectra], adjoint_hat, final_table)


def solution(mesh):
    spec = P(None, None, "wide", "narrow", None)
    return jax.shard_map(
        functools.partial(local, mesh.shape["wide"], mesh.shape["narrow"]),
        mesh=mesh,
        in_specs=(spec, spec),
        out_specs=spec,
        check_vma=False,
    )
```

```python
import functools
import math

import jax
import jax.numpy as jnp
import ml_dtypes
import numpy as np
from jax import lax
from jax.experimental import pallas as pl
from jax.experimental.pallas import tpu as pltpu
from jax.sharding import PartitionSpec as P

NX = 512
NY = 256
NZ = 256
KX = 256

section_step = 0.25
viscous_rate = 0.05
axes = ("wide", "narrow")
VMEM_LIMIT = 60 * 2**20


def signed(count):
    number = np.arange(count)
    return np.where(number < count // 2, number, number - count).astype(np.float64)


def phases(modes, places, length):
    angle = 2.0 * math.pi / length * (np.outer(np.arange(modes), np.arange(places)) % length)
    return np.cos(angle), np.sin(angle)


def split_table(table):
    table = np.asarray(table, np.float32)
    high = table.astype(ml_dtypes.bfloat16)
    low = (table - high.astype(np.float32)).astype(ml_dtypes.bfloat16)
    return np.stack([high, low], 0)


def split(value):
    high = value.astype(jnp.bfloat16)
    return high, (value - high.astype(jnp.float32)).astype(jnp.bfloat16)


def product(left, right, dims):
    def one(first, second):
        return lax.dot_general(first, second, (dims, ((), ())), preferred_element_type=jnp.float32)

    return one(left[1], right[0]) + one(left[0], right[1]) + one(left[0], right[0])


def table_parts(ref):
    return ref[0], ref[1]


PLAIN = ((1,), (0,))
BOTH_MINOR = ((1,), (1,))


def whole_spec(shape):
    return pl.BlockSpec(shape, lambda *_: (0,) * len(shape), pipeline_mode=pl.Buffered(1))


def params():
    return pltpu.CompilerParams(vmem_limit_bytes=VMEM_LIMIT)


def cost(flops, moved):
    return pl.CostEstimate(flops=int(flops), bytes_accessed=int(moved), transcendentals=0)


def depth_kernel(tables_count, by_owner, field_ref, *refs):
    tables, outs = refs[:tables_count], refs[tables_count:]
    for row in range(field_ref.shape[2]):
        real, imag = field_ref[0, 0, row], field_ref[0, 1, row]
        first = jnp.concatenate([real, imag], 0)
        second = jnp.concatenate([-imag, real], 0)
        rows = split(jnp.concatenate([first, second], 1))
        for table, out in zip(tables, outs):
            value = product(table_parts(table), rows, BOTH_MINOR)
            if by_owner:
                out[:, row] = value.reshape(out.shape[0], out.shape[2], out.shape[3])
            else:
                out[row] = value


def depth(field, member, tables, owners):
    rows_x, rows_y = field.shape[2], field.shape[3]
    block = NZ // owners
    lanes = 2 * rows_y
    tile = min(8, rows_x)
    by_owner = block % 8 == 0
    if by_owner:
        shape = (owners, rows_x, block, lanes)
        spec = pl.BlockSpec((owners, tile, block, lanes), lambda i: (0, i, 0, 0))
    else:
        shape = (rows_x, NZ, lanes)
        spec = pl.BlockSpec((tile, NZ, lanes), lambda i: (i, 0, 0))
    count = len(tables)
    outs = pl.pallas_call(
        functools.partial(depth_kernel, count, by_owner),
        grid=(rows_x // tile,),
        in_specs=[pl.BlockSpec((1, 2, tile, rows_y, NZ), lambda i: (member, 0, i, 0, 0))]
        + [whole_spec(t.shape) for t in tables],
        out_specs=[spec] * count,
        out_shape=[jax.ShapeDtypeStruct(shape, jnp.float32)] * count,
        compiler_params=params(),
        cost_estimate=cost(6.0 * count * rows_x * lanes * NZ * 2 * NZ, 4 * (count + 1) * rows_x * lanes * NZ),
        name="depth_synthesis",
    )(field, *tables)
    if not by_owner:
        outs = [o.reshape(rows_x, owners, block, lanes).transpose(1, 0, 2, 3) for o in outs]
    return outs


def exchange(value):
    return lax.all_to_all(value, axes, split_axis=0, concat_axis=0, tiled=True)


def plane_rows(ref, narrow, block, plane):
    owners, rows, lanes = ref.shape
    value = ref[:, pl.ds(plane, rows // block, stride=block), :]
    value = value.reshape(owners // narrow, narrow, rows // block, lanes)
    pieces = [value[:, n].reshape(KX, lanes) for n in range(narrow)]
    return split(jnp.concatenate(pieces, 1))


def stacked(value):
    return jnp.concatenate([value[:, :NY], value[:, NY:]], 0)


def times_i(value):
    return jnp.concatenate([-value[:, NY:], value[:, :NY]], 1)


def lines(value, synth):
    return product(table_parts(synth), split(stacked(value)), PLAIN)


def velocity_kernel(narrow, block, *refs):
    ux, uy, uz, dzux, dzuy, span, slope, synth = refs[:8]
    outs = refs[8:]
    plane = pl.program_id(0)
    wave = lax.broadcasted_iota(jnp.int32, (KX, 2 * NY), 0).astype(jnp.float32) * (2.0 * math.pi / NX)

    def rows(ref):
        return plane_rows(ref, narrow, block, plane)

    def to_y(value, table):
        return product(value, table_parts(table), PLAIN)

    rows_x = rows(ux)
    value_x = to_y(rows_x, span)
    outs[0][0] = lines(value_x, synth)
    value_y = to_y(rows(uy), span)
    outs[1][0] = lines(value_y, synth)
    rows_z = rows(uz)
    value_z = to_y(rows_z, span)
    outs[2][0] = lines(value_z, synth)
    outs[3][0] = lines(to_y(rows_z, slope) - to_y(rows(dzuy), span), synth)
    outs[4][0] = lines(to_y(rows(dzux), span) - wave * times_i(value_z), synth)
    outs[5][0] = lines(wave * times_i(value_y) - to_y(rows_x, slope), synth)


def adjoint_kernel(narrow, block, field, span, synth, out):
    rows = plane_rows(field, narrow, block, pl.program_id(0))
    out[0] = lines(product(rows, table_parts(span), PLAIN), synth)


def physical_call(kernel, name, fields, tables, count, narrow):
    owners, rows_x, block, lanes = fields[0].shape
    fields = [f.reshape(owners, rows_x * block, lanes) for f in fields]
    spec = pl.BlockSpec((1, NX, NY), lambda z: (z, 0, 0))
    return pl.pallas_call(
        functools.partial(kernel, narrow, block),
        grid=(block,),
        in_specs=[whole_spec(f.shape) for f in fields] + [whole_spec(t.shape) for t in tables],
        out_specs=[spec] * count,
        out_shape=[jax.ShapeDtypeStruct((block, NX, NY), jnp.float32)] * count,
        compiler_params=params(),
        cost_estimate=cost(12.0 * count * block * KX * 4 * NY * NY, 4 * 2 * count * block * NX * NY),
        name=name,
    )(*fields, *tables)


def analysis_kernel(kept, rows_x, narrow, transport, *refs):
    a = [r[0] for r in refs[0:3]]
    u = [r[0] for r in refs[3:6]]
    o = [r[0] for r in refs[6:9]]
    anal, span, slope = refs[9:12]
    outs = refs[12:]
    wave = lax.broadcasted_iota(jnp.int32, (kept, 2 * NY), 0).astype(jnp.float32) * (2.0 * math.pi / NX)

    def cross(p, q, c):
        d, e = (c + 1) % 3, (c + 2) % 3
        return p[d] * q[e] - p[e] * q[d]

    def modes(cells):
        value = product(table_parts(anal), split(cells), PLAIN)
        return jnp.concatenate([value[:kept], value[kept:]], 1)

    def to_y(value, table):
        return product(split(value), table_parts(table), PLAIN)

    def pack(value, rows):
        return jnp.concatenate([value[:rows], value[rows:]], 1)

    def store(out, value):
        lanes = value.shape[1] // narrow
        half, part = rows_x // 2, rows_x // 4
        for w in range(kept // rows_x):
            for n in range(narrow):
                owner = 0 if n < narrow // 2 else narrow - 1
                block = value[w * rows_x : (w + 1) * rows_x]
                near = block[:, n * lanes : n * lanes + lanes // 2]
                far = block[:, owner * lanes + lanes // 2 : (owner + 1) * lanes]
                far = far[(n % 2) * half : (n % 2 + 1) * half]
                out[w * narrow + n, 0] = jnp.concatenate(
                    [pack(near[:half], part), pack(near[half:], part), pack(far, part)], 0
                )
        for d in range(kept // rows_x * narrow, out.shape[0]):
            out[d, 0] = jnp.zeros(out.shape[2:], jnp.float32)

    if transport:
        for c in range(2):
            store(outs[c], to_y(modes(cross(u, a, c)), span))
        return
    tx, ty, tz = [modes(cross(u, a, c)) for c in range(3)]
    store(outs[0], to_y(modes(cross(a, o, 0)), span) + to_y(tz, slope))
    store(outs[1], to_y(modes(cross(a, o, 1)) - wave * times_i(tz), span))
    store(outs[2], to_y(modes(cross(a, o, 2)) + wave * times_i(ty), span) - to_y(tx, slope))


def analysis(fields, tables, kept, rows_x, wide, narrow, transport):
    block = fields[0].shape[0]
    owners = wide * narrow
    lanes = 2 * NY // narrow
    rows = rows_x * 3 // 4
    count = 2 if transport else 3
    spec = pl.BlockSpec((1, NX, NY), lambda z: (z, 0, 0))
    out = pl.BlockSpec((owners, 1, rows, lanes), lambda z: (0, z, 0, 0))
    return pl.pallas_call(
        functools.partial(analysis_kernel, kept, rows_x, narrow, transport),
        grid=(block,),
        in_specs=[spec] * 9 + [whole_spec(t.shape) for t in tables],
        out_specs=[out] * count,
        out_shape=[jax.ShapeDtypeStruct((owners, block, rows, lanes), jnp.float32)] * count,
        compiler_params=params(),
        cost_estimate=cost(6.0 * block * 4 * count * kept * 2 * NX * NY, 4 * 12 * block * NX * NY),
        name="transport_analysis" if transport else "products_and_analysis",
    )(*fields, *tables)


def final_kernel(narrow, *refs):
    nears, owns, others = refs[0:5], refs[5:10], refs[10:15]
    adjoint, table, out = refs[15:]
    group, side = pl.program_id(0) // 2, pl.program_id(0) % 2
    lower = lax.axis_index("narrow") < narrow // 2
    use_own = lower == (group == 0)
    tile, rows_y = adjoint.shape[2], adjoint.shape[3]
    first_x = lax.axis_index("wide") * (tile * pl.num_programs(0)) + pl.program_id(0) * tile
    shape = (rows_y, NZ)
    number_y = lax.broadcasted_iota(jnp.int32, shape, 0) + lax.axis_index("narrow") * rows_y
    number_y = jnp.where(number_y < NY // 2, number_y, number_y - NY)
    number_z = lax.broadcasted_iota(jnp.int32, shape, 1)
    number_z = jnp.where(number_z < NZ // 2, number_z, number_z - NZ)
    keep_yz = (3 * jnp.abs(number_y) < NY) & (3 * jnp.abs(number_z) < NZ)
    ky = number_y.astype(jnp.float32) * (2.0 * math.pi / NY)
    kz = number_z.astype(jnp.float32) * (2.0 * math.pi / NZ)
    for row in range(tile):
        parts = []
        for near, own, other in zip(nears, owns, others):
            near, own, other = [
                r.reshape(NZ * tile, 2 * rows_y)[pl.ds(row, NZ, stride=tile), :] for r in (near, own, other)
            ]
            far = jnp.where(use_own, own, other)
            first, second = jnp.where(lower, near, far), jnp.where(lower, far, near)
            cells = jnp.where(
                side == 0,
                jnp.concatenate([first[:, :rows_y], second[:, :rows_y]], 1),
                jnp.concatenate([first[:, rows_y:], second[:, rows_y:]], 1),
            ).T
            both = product(split(cells), table_parts(table), PLAIN)
            quarter = rows_y // 2
            real, imag = [
                jnp.concatenate([both[p * quarter : (p + 1) * quarter], both[(p + 2) * quarter : (p + 3) * quarter]], 0)
                for p in range(2)
            ]
            parts.append((real[:, :NZ] + imag[:, NZ:], imag[:, :NZ] - real[:, NZ:]))
        number_x = jnp.full(shape, first_x + row, jnp.int32)
        kx = number_x.astype(jnp.float32) * (2.0 * math.pi / NX)
        ksquare = kx * kx + ky * ky + kz * kz
        inverse = 1.0 / (ksquare + (ksquare == 0).astype(jnp.float32))
        keep = (keep_yz & (3 * number_x < NX)).astype(jnp.float32) * section_step
        decay = jnp.exp(-viscous_rate * ksquare)
        a1, a2, a3, t1, t2 = parts
        real = (a1[0] + kz * t2[1], a2[0] - kz * t1[1], a3[0])
        imag = (a1[1] - kz * t2[0], a2[1] + kz * t1[0], a3[1])
        for part, conv in enumerate((real, imag)):
            along = (kx * conv[0] + ky * conv[1] + kz * conv[2]) * inverse
            for c, wave in enumerate((kx, ky, kz)):
                out[c, part, row] = decay * (adjoint[c, part, row] + keep * (conv[c] - wave * along))


def final(spectra, adjoint_hat, table, narrow):
    rows_x, rows_y = adjoint_hat.shape[2], adjoint_hat.shape[3]
    tile, lanes = rows_x // 4, 2 * rows_y
    nears, owns, others = [], [], []
    for s in spectra:
        nears.append(s[:, :, : 2 * tile].reshape(NZ, 2, tile, lanes))
        own = s[:, :, 2 * tile :].reshape(NZ, tile, lanes)
        owns.append(own)
        others.append(lax.ppermute(own, "narrow", [(1, 0), (narrow - 2, narrow - 1)]))
    hat = pl.BlockSpec((3, 2, tile, rows_y, NZ), lambda i: (0, 0, i, 0, 0))
    near = pl.BlockSpec((NZ, 1, tile, lanes), lambda i: (0, i // 2, 0, 0))
    return pl.pallas_call(
        functools.partial(final_kernel, narrow),
        grid=(4,),
        in_specs=[near] * 5 + [whole_spec((NZ, tile, lanes))] * 10 + [hat, whole_spec(table.shape)],
        out_specs=hat,
        out_shape=jax.ShapeDtypeStruct(adjoint_hat.shape, jnp.float32),
        compiler_params=params(),
        cost_estimate=cost(30.0 * rows_x * 2 * rows_y * NZ * 2 * NZ, 4 * 22 * rows_x * rows_y * NZ),
        name="depth_analysis_projection",
    )(*nears, *owns, *others, adjoint_hat, table)


def local(wide, narrow, adjoint_hat, velocity_hat):
    owners = wide * narrow
    rows_x, rows_y = adjoint_hat.shape[2], adjoint_hat.shape[3]
    kept = -(-(-(-NX // 3)) // rows_x) * rows_x
    scale = 1.0 / math.sqrt(NX * NY * NZ)
    cosine, sine = phases(NZ, NZ, NZ)
    wave_z = 2.0 * math.pi / NZ * signed(NZ)[None, :]
    depth_table = split_table(np.concatenate([cosine, sine], 1))
    depth_slope = split_table(np.concatenate([-wave_z * sine, wave_z * cosine], 1))
    final_table = split_table(np.concatenate([cosine, sine], 1))
    cosine, sine = phases(NY, NY, NY)
    wave_y = 2.0 * math.pi / NY * signed(NY)[:, None]

    def merged(real, imag):
        return np.stack([np.stack([real, imag], 1), np.stack([-imag, real], 1)], 0)

    def rows_first(real, imag):
        table = merged(real, imag).reshape(2, narrow, rows_y, 2, NY)
        return split_table(table.transpose(1, 0, 2, 3, 4).reshape(2 * NY, 2 * NY))

    def rows_last(real, imag):
        table = merged(real, imag).transpose(0, 3, 2, 1).reshape(2, NY, 2, narrow, 2, rows_y // 2)
        table = table.transpose(0, 1, 3, 4, 2, 5)
        upper = table[:, :, narrow // 2 :, ::-1]
        table = np.concatenate([table[:, :, : narrow // 2], upper], 2)
        return split_table(table.reshape(2 * NY, 2 * NY))

    span = rows_first(cosine, sine)
    slope = rows_first(-wave_y * sine, wave_y * cosine)
    back_span = rows_last(cosine, -sine)
    back_slope = rows_last(wave_y * sine, wave_y * cosine)
    cosine, sine = phases(KX, NX, NX)
    weights = np.where(np.arange(KX) == 0, 1.0, 2.0)[:, None] * scale
    synth = split_table(np.concatenate([cosine * weights, -sine * weights], 0).T)
    anal = split_table(np.concatenate([cosine[:kept], -sine[:kept]], 0) * scale)

    buffers = depth(velocity_hat, 2, [depth_table], owners)
    buffers += depth(velocity_hat, 0, [depth_table, depth_slope], owners)
    buffers += depth(velocity_hat, 1, [depth_table, depth_slope], owners)
    for c in range(3):
        buffers += depth(adjoint_hat, c, [depth_table], owners)
    arrived = []
    for place, buffer in enumerate(buffers):
        if place == 7:
            uz, ux, dzux, uy, dzuy = arrived[:5]
            flow = physical_call(
                velocity_kernel, "velocity_lines", [ux, uy, uz, dzux, dzuy], [span, slope, synth], 6, narrow
            )
            buffer, flow = lax.optimization_barrier((buffer, flow))
        if arrived:
            buffer, arrived[-1] = lax.optimization_barrier((buffer, arrived[-1]))
        arrived.append(exchange(buffer))
    hats = arrived[5:]
    adjoint = [
        physical_call(adjoint_kernel, "adjoint_lines", [hat], [span, synth], 1, narrow)[0] for hat in hats
    ]
    fields, tables = adjoint + list(flow), [anal, back_span, back_slope]
    transport, curled = [analysis(fields, tables, kept, rows_x, wide, narrow, t) for t in (True, False)]
    first = exchange(transport[0])
    second, curled = lax.optimization_barrier((transport[1], curled))
    spectra = [exchange(s) for s in curled] + [first, exchange(second)]
    return final(spectra, adjoint_hat, final_table, narrow)


def solution(mesh):
    spec = P(None, None, "wide", "narrow", None)
    return jax.shard_map(
        functools.partial(local, mesh.shape["wide"], mesh.shape["narrow"]),
        mesh=mesh,
        in_specs=(spec, spec),
        out_specs=spec,
        check_vma=False,
    )
```

```python
import functools
import math

import jax
import jax.numpy as jnp
import ml_dtypes
import numpy as np
from jax import lax
from jax.experimental import pallas as pl
from jax.experimental.pallas import tpu as pltpu
from jax.sharding import PartitionSpec as P

NX = 512
NY = 256
NZ = 256
KX = 256

section_step = 0.25
viscous_rate = 0.05
axes = ("wide", "narrow")
VMEM_LIMIT = 60 * 2**20


def signed(count):
    number = np.arange(count)
    return np.where(number < count // 2, number, number - count).astype(np.float64)


def phases(modes, places, length):
    angle = 2.0 * math.pi / length * (np.outer(np.arange(modes), np.arange(places)) % length)
    return np.cos(angle), np.sin(angle)


def split_table(table):
    table = np.asarray(table, np.float32)
    high = table.astype(ml_dtypes.bfloat16)
    low = (table - high.astype(np.float32)).astype(ml_dtypes.bfloat16)
    return np.stack([high, low], 0)


def split(value):
    high = value.astype(jnp.bfloat16)
    return high, (value - high.astype(jnp.float32)).astype(jnp.bfloat16)


def product(left, right, dims):
    def one(first, second):
        return lax.dot_general(first, second, (dims, ((), ())), preferred_element_type=jnp.float32)

    return one(left[1], right[0]) + one(left[0], right[1]) + one(left[0], right[0])


def table_parts(ref):
    return ref[0], ref[1]


PLAIN = ((1,), (0,))
BOTH_MINOR = ((1,), (1,))


def whole_spec(shape):
    return pl.BlockSpec(shape, lambda *_: (0,) * len(shape), pipeline_mode=pl.Buffered(1))


def params():
    return pltpu.CompilerParams(vmem_limit_bytes=VMEM_LIMIT)


def cost(flops, moved):
    return pl.CostEstimate(flops=int(flops), bytes_accessed=int(moved), transcendentals=0)


def depth_kernel(tables_count, by_owner, field_ref, *refs):
    tables, outs = refs[:tables_count], refs[tables_count:]
    for row in range(field_ref.shape[2]):
        real, imag = field_ref[0, 0, row], field_ref[0, 1, row]
        first = jnp.concatenate([real, imag], 0)
        second = jnp.concatenate([-imag, real], 0)
        rows = split(jnp.concatenate([first, second], 1))
        for table, out in zip(tables, outs):
            value = product(table_parts(table), rows, BOTH_MINOR)
            if by_owner:
                out[:, row] = value.reshape(out.shape[0], out.shape[2], out.shape[3])
            else:
                out[row] = value


def depth(field, member, tables, owners):
    rows_x, rows_y = field.shape[2], field.shape[3]
    block = NZ // owners
    lanes = 2 * rows_y
    tile = min(8, rows_x)
    by_owner = block % 8 == 0
    if by_owner:
        shape = (owners, rows_x, block, lanes)
        spec = pl.BlockSpec((owners, tile, block, lanes), lambda i: (0, i, 0, 0))
    else:
        shape = (rows_x, NZ, lanes)
        spec = pl.BlockSpec((tile, NZ, lanes), lambda i: (i, 0, 0))
    count = len(tables)
    outs = pl.pallas_call(
        functools.partial(depth_kernel, count, by_owner),
        grid=(rows_x // tile,),
        in_specs=[pl.BlockSpec((1, 2, tile, rows_y, NZ), lambda i: (member, 0, i, 0, 0))]
        + [whole_spec(t.shape) for t in tables],
        out_specs=[spec] * count,
        out_shape=[jax.ShapeDtypeStruct(shape, jnp.float32)] * count,
        compiler_params=params(),
        cost_estimate=cost(6.0 * count * rows_x * lanes * NZ * 2 * NZ, 4 * (count + 1) * rows_x * lanes * NZ),
        name="depth_synthesis",
    )(field, *tables)
    if not by_owner:
        outs = [o.reshape(rows_x, owners, block, lanes).transpose(1, 0, 2, 3) for o in outs]
    return outs


def exchange(value):
    return lax.all_to_all(value, axes, split_axis=0, concat_axis=0, tiled=True)


def plane_rows(ref, narrow, block, plane):
    owners, rows, lanes = ref.shape
    value = ref[:, pl.ds(plane, rows // block, stride=block), :]
    value = value.reshape(owners // narrow, narrow, rows // block, lanes)
    pieces = [value[:, n].reshape(KX, lanes) for n in range(narrow)]
    return split(jnp.concatenate(pieces, 1))


def stacked(value):
    return jnp.concatenate([value[:, :NY], value[:, NY:]], 0)


def times_i(value):
    return jnp.concatenate([-value[:, NY:], value[:, :NY]], 1)


def lines(value, synth):
    return product(table_parts(synth), split(stacked(value)), PLAIN)


def vorticity_kernel(narrow, block, *refs):
    ux, uy, uz, dzux, dzuy, span, slope, synth = refs[:8]
    outs = refs[8:]
    plane = pl.program_id(0)
    wave = lax.broadcasted_iota(jnp.int32, (KX, 2 * NY), 0).astype(jnp.float32) * (2.0 * math.pi / NX)

    def rows(ref):
        return plane_rows(ref, narrow, block, plane)

    def to_y(value, table):
        return product(value, table_parts(table), PLAIN)

    rows_x, rows_z = rows(ux), rows(uz)
    value_y, value_z = to_y(rows(uy), span), to_y(rows_z, span)
    outs[0][0] = lines(to_y(rows_z, slope) - to_y(rows(dzuy), span), synth)
    outs[1][0] = lines(to_y(rows(dzux), span) - wave * times_i(value_z), synth)
    outs[2][0] = lines(wave * times_i(value_y) - to_y(rows_x, slope), synth)


def field_kernel(narrow, block, field, span, synth, out):
    rows = plane_rows(field, narrow, block, pl.program_id(0))
    out[0] = lines(product(rows, table_parts(span), PLAIN), synth)


def physical_call(kernel, name, fields, tables, count, narrow):
    owners, rows_x, block, lanes = fields[0].shape
    fields = [f.reshape(owners, rows_x * block, lanes) for f in fields]
    spec = pl.BlockSpec((1, NX, NY), lambda z: (z, 0, 0))
    return pl.pallas_call(
        functools.partial(kernel, narrow, block),
        grid=(block,),
        in_specs=[whole_spec(f.shape) for f in fields] + [whole_spec(t.shape) for t in tables],
        out_specs=[spec] * count,
        out_shape=[jax.ShapeDtypeStruct((block, NX, NY), jnp.float32)] * count,
        compiler_params=params(),
        cost_estimate=cost(12.0 * count * block * KX * 4 * NY * NY, 4 * 2 * count * block * NX * NY),
        name=name,
    )(*fields, *tables)


def analysis_kernel(kept, rows_x, narrow, transport, *refs):
    a = [r[0] for r in refs[0:3]]
    u = [r[0] for r in refs[3:6]]
    o = [] if transport else [r[0] for r in refs[6:9]]
    anal, span, slope = refs[6 + len(o) : 9 + len(o)]
    outs = refs[9 + len(o) :]
    wave = lax.broadcasted_iota(jnp.int32, (kept, 2 * NY), 0).astype(jnp.float32) * (2.0 * math.pi / NX)

    def cross(p, q, c):
        d, e = (c + 1) % 3, (c + 2) % 3
        return p[d] * q[e] - p[e] * q[d]

    def modes(cells):
        value = product(table_parts(anal), split(cells), PLAIN)
        return jnp.concatenate([value[:kept], value[kept:]], 1)

    def to_y(value, table):
        return product(split(value), table_parts(table), PLAIN)

    def pack(value, rows):
        return jnp.concatenate([value[:rows], value[rows:]], 1)

    def store(out, value):
        lanes = value.shape[1] // narrow
        half, part = rows_x // 2, rows_x // 4
        for w in range(kept // rows_x):
            for n in range(narrow):
                owner = 0 if n < narrow // 2 else narrow - 1
                block = value[w * rows_x : (w + 1) * rows_x]
                near = block[:, n * lanes : n * lanes + lanes // 2]
                far = block[:, owner * lanes + lanes // 2 : (owner + 1) * lanes]
                far = far[(n % 2) * half : (n % 2 + 1) * half]
                out[w * narrow + n, 0] = jnp.concatenate(
                    [pack(near[:half], part), pack(near[half:], part), pack(far, part)], 0
                )
        for d in range(kept // rows_x * narrow, out.shape[0]):
            out[d, 0] = jnp.zeros(out.shape[2:], jnp.float32)

    if transport:
        for c in range(2):
            store(outs[c], to_y(modes(cross(u, a, c)), span))
        return
    tx, ty, tz = [modes(cross(u, a, c)) for c in range(3)]
    store(outs[0], to_y(modes(cross(a, o, 0)), span) + to_y(tz, slope))
    store(outs[1], to_y(modes(cross(a, o, 1)) - wave * times_i(tz), span))
    store(outs[2], to_y(modes(cross(a, o, 2)) + wave * times_i(ty), span) - to_y(tx, slope))


def analysis(fields, tables, kept, rows_x, wide, narrow, transport):
    block = fields[0].shape[0]
    owners = wide * narrow
    lanes = 2 * NY // narrow
    rows = rows_x * 3 // 4
    count = 2 if transport else 3
    spec = pl.BlockSpec((1, NX, NY), lambda z: (z, 0, 0))
    out = pl.BlockSpec((owners, 1, rows, lanes), lambda z: (0, z, 0, 0))
    return pl.pallas_call(
        functools.partial(analysis_kernel, kept, rows_x, narrow, transport),
        grid=(block,),
        in_specs=[spec] * len(fields) + [whole_spec(t.shape) for t in tables],
        out_specs=[out] * count,
        out_shape=[jax.ShapeDtypeStruct((owners, block, rows, lanes), jnp.float32)] * count,
        compiler_params=params(),
        cost_estimate=cost(6.0 * block * 4 * count * kept * 2 * NX * NY, 4 * 12 * block * NX * NY),
        name="transport_analysis" if transport else "products_and_analysis",
    )(*fields, *tables)


def final_kernel(narrow, *refs):
    nears, owns, others = refs[0:5], refs[5:10], refs[10:15]
    adjoint, table, out = refs[15:]
    count, rows_y = adjoint.shape[4], adjoint.shape[5]
    tile, lanes = nears[0].shape[2], nears[0].shape[3]
    group, step = pl.program_id(0), pl.program_id(1)
    lower = lax.axis_index("narrow") < narrow // 2
    use_own = lower == (group == 0)
    first_x = lax.axis_index("wide") * (4 * tile) + group * 2 * tile + step * count
    shape = (rows_y, NZ)
    number_y = lax.broadcasted_iota(jnp.int32, shape, 0) + lax.axis_index("narrow") * rows_y
    number_y = jnp.where(number_y < NY // 2, number_y, number_y - NY)
    number_z = lax.broadcasted_iota(jnp.int32, shape, 1)
    number_z = jnp.where(number_z < NZ // 2, number_z, number_z - NZ)
    keep_yz = (3 * jnp.abs(number_y) < NY) & (3 * jnp.abs(number_z) < NZ)
    ky = number_y.astype(jnp.float32) * (2.0 * math.pi / NY)
    kz = number_z.astype(jnp.float32) * (2.0 * math.pi / NZ)
    quarter = rows_y // 2

    def modes(ref_values):
        return product(split(ref_values.T), table_parts(table), PLAIN)

    for row in range(count):
        pairs = []
        for refs_of in zip(nears, owns, others):
            near, own, other = [
                r.reshape(NZ * tile, lanes)[pl.ds(step * count + row, NZ, stride=tile), :] for r in refs_of
            ]
            far = jnp.where(use_own, own, other)
            pairs.append((modes(jnp.where(lower, near, far)), modes(jnp.where(lower, far, near))))
        for side in range(2):
            parts = []
            for first, second in pairs:
                real, imag = [
                    jnp.concatenate([v[at : at + quarter] for v in (first, second)], 0)
                    for at in (side * rows_y, side * rows_y + quarter)
                ]
                parts.append((real[:, :NZ] + imag[:, NZ:], imag[:, :NZ] - real[:, NZ:]))
            number_x = jnp.full(shape, first_x + side * tile + row, jnp.int32)
            kx = number_x.astype(jnp.float32) * (2.0 * math.pi / NX)
            ksquare = kx * kx + ky * ky + kz * kz
            inverse = 1.0 / (ksquare + (ksquare == 0).astype(jnp.float32))
            keep = (keep_yz & (3 * number_x < NX)).astype(jnp.float32) * section_step
            decay = jnp.exp(-viscous_rate * ksquare)
            a1, a2, a3, t1, t2 = parts
            real = (a1[0] + kz * t2[1], a2[0] - kz * t1[1], a3[0])
            imag = (a1[1] - kz * t2[0], a2[1] + kz * t1[0], a3[1])
            for part, conv in enumerate((real, imag)):
                along = (kx * conv[0] + ky * conv[1] + kz * conv[2]) * inverse
                for c, wave in enumerate((kx, ky, kz)):
                    old = adjoint[c, part, 0, side, row]
                    out[c, part, 0, side, row] = decay * (old + keep * (conv[c] - wave * along))


def final(spectra, adjoint_hat, table, narrow):
    rows_x, rows_y = adjoint_hat.shape[2], adjoint_hat.shape[3]
    tile, lanes = rows_x // 4, 2 * rows_y
    count = min(2, tile)
    spectra = [s.reshape(NZ, 3, tile, lanes) for s in spectra]
    others = [lax.ppermute(s[:, 2], "narrow", [(1, 0), (narrow - 2, narrow - 1)]) for s in spectra]
    paired = (3, 2, 2, 2, tile, rows_y, NZ)
    hat = pl.BlockSpec((3, 2, 1, 2, count, rows_y, NZ), lambda g, i: (0, 0, g, 0, i, 0, 0))
    near = pl.BlockSpec((NZ, 1, tile, lanes), lambda g, i: (0, g, 0, 0))
    own = pl.BlockSpec((NZ, 1, tile, lanes), lambda g, i: (0, 2, 0, 0), pipeline_mode=pl.Buffered(1))
    result = pl.pallas_call(
        functools.partial(final_kernel, narrow),
        grid=(2, tile // count),
        in_specs=[near] * 5 + [own] * 5 + [whole_spec((NZ, tile, lanes))] * 5 + [hat, whole_spec(table.shape)],
        out_specs=hat,
        out_shape=jax.ShapeDtypeStruct(paired, jnp.float32),
        compiler_params=params(),
        cost_estimate=cost(30.0 * rows_x * 2 * rows_y * NZ * 2 * NZ, 4 * 22 * rows_x * rows_y * NZ),
        name="depth_analysis_projection",
    )(*spectra, *spectra, *others, adjoint_hat.reshape(paired), table)
    return result.reshape(adjoint_hat.shape)


def local(wide, narrow, adjoint_hat, velocity_hat):
    owners = wide * narrow
    rows_x, rows_y = adjoint_hat.shape[2], adjoint_hat.shape[3]
    kept = -(-(-(-NX // 3)) // rows_x) * rows_x
    scale = 1.0 / math.sqrt(NX * NY * NZ)
    cosine, sine = phases(NZ, NZ, NZ)
    wave_z = 2.0 * math.pi / NZ * signed(NZ)[None, :]
    depth_table = split_table(np.concatenate([cosine, sine], 1))
    depth_slope = split_table(np.concatenate([-wave_z * sine, wave_z * cosine], 1))
    final_table = split_table(np.concatenate([cosine, sine], 1))
    cosine, sine = phases(NY, NY, NY)
    wave_y = 2.0 * math.pi / NY * signed(NY)[:, None]

    def merged(real, imag):
        return np.stack([np.stack([real, imag], 1), np.stack([-imag, real], 1)], 0)

    def rows_first(real, imag):
        table = merged(real, imag).reshape(2, narrow, rows_y, 2, NY)
        return split_table(table.transpose(1, 0, 2, 3, 4).reshape(2 * NY, 2 * NY))

    def rows_last(real, imag):
        table = merged(real, imag).transpose(0, 3, 2, 1).reshape(2, NY, 2, narrow, 2, rows_y // 2)
        table = table.transpose(0, 1, 3, 4, 2, 5)
        upper = table[:, :, narrow // 2 :, ::-1]
        table = np.concatenate([table[:, :, : narrow // 2], upper], 2)
        return split_table(table.reshape(2 * NY, 2 * NY))

    span = rows_first(cosine, sine)
    slope = rows_first(-wave_y * sine, wave_y * cosine)
    back_span = rows_last(cosine, -sine)
    back_slope = rows_last(wave_y * sine, wave_y * cosine)
    cosine, sine = phases(KX, NX, NX)
    weights = np.where(np.arange(KX) == 0, 1.0, 2.0)[:, None] * scale
    synth = split_table(np.concatenate([cosine * weights, -sine * weights], 0).T)
    anal = split_table(np.concatenate([cosine[:kept], -sine[:kept]], 0) * scale)

    (bz,) = depth(velocity_hat, 2, [depth_table], owners)
    bx, dx = depth(velocity_hat, 0, [depth_table, depth_slope], owners)
    by, dy = depth(velocity_hat, 1, [depth_table, depth_slope], owners)
    buffers = [bz, bx, by] + [depth(adjoint_hat, c, [depth_table], owners)[0] for c in range(3)]

    def tie(*values):
        return lax.optimization_barrier(values)

    def field_lines(value):
        return physical_call(field_kernel, "field_lines", [value], [span, synth], 1, narrow)[0]

    arrived, cells = [], []
    for buffer in buffers:
        if len(arrived) >= 2:
            cells.append(field_lines(arrived[-2]))
            buffer, cells[-1] = tie(buffer, cells[-1])
        if arrived:
            buffer, arrived[-1] = tie(buffer, arrived[-1])
        arrived.append(exchange(buffer))
    dx, arrived[5], last = tie(dx, arrived[5], field_lines(arrived[4]))
    cells.append(last)
    dzux = exchange(dx)
    cells.append(field_lines(arrived[5]))
    fields = cells[3:6] + [cells[1], cells[2], cells[0]]
    tables = [anal, back_span, back_slope]
    transport = analysis(fields, tables, kept, rows_x, wide, narrow, True)
    dy, dzux, first, second = tie(dy, dzux, *transport)
    dzuy = exchange(dy)
    first, dzuy = tie(first, dzuy)
    first = exchange(first)
    flow = [arrived[1], arrived[2], arrived[0], dzux, dzuy]
    curl = physical_call(vorticity_kernel, "vorticity_lines", flow, [span, slope, synth], 3, narrow)
    second, first, *curl = tie(second, first, *curl)
    second = exchange(second)
    curled = analysis(fields + list(curl), tables, kept, rows_x, wide, narrow, False)
    second, *curled = tie(second, *curled)
    spectra = [exchange(c) for c in curled] + [first, second]
    return final(spectra, adjoint_hat, final_table, narrow)


def solution(mesh):
    spec = P(None, None, "wide", "narrow", None)
    return jax.shard_map(
        functools.partial(local, mesh.shape["wide"], mesh.shape["narrow"]),
        mesh=mesh,
        in_specs=(spec, spec),
        out_specs=spec,
        check_vma=False,
    )
```
